128 devices in a mesh: dom: 32 (over z, x, core), sub: 4 (over y).
Axes of the slice: x: 4, y: 4, z: 4, core: 2. Of those that a mesh axis runs over, the one named last changes fastest.
Arguments:
- primal: bfloat16 [5, 64, 262144], P(None, None, ('dom', 'sub'))
- adjoint: bfloat16 [5, 64, 262144], P(None, None, ('dom', 'sub')), may hold values from -5 to 5
- order: int32 [262144], P(('dom', 'sub')), may hold values from 1 to 3
- faces_nbr: int32 [6, 262144], P(None, ('dom', 'sub')), may hold values from -1 to 2559, as said below
- move_elem: int32 [32768], P(('dom', 'sub')), may hold values from 0 to 2047, as said below
- move_dest: int32 [32768, 1], P(('dom', 'sub')), may hold values from 0 to 127; in each aligned block of 256 rows (0 to 255, 256 to 511, ...) at most 4 rows name the same one
- eval_op: bfloat16 [216, 64], replicated, may hold values from -0.75 to 0.75
- gradient_operator: bfloat16 [3, 125, 216], replicated, may hold values from -0.25 to 0.25
- flux_jac: float32 [3, 5, 5], replicated, may hold values from -2.5 to 2.5
- trace_op: bfloat16 [6, 16, 64], replicated, may hold values from -0.75 to 0.75
- lifting_operator: bfloat16 [6, 125, 16], replicated, may hold values from -0.625 to 0.625
- patch_from_self: bfloat16 [125, 64], replicated, may hold values from -0.75 to 0.75
- patch_from_faces: bfloat16 [6, 125, 16], replicated, may hold values from -0.625 to 0.625
Outputs:
- indicator: float32 [262144], P(('dom', 'sub'))
- shipped_adjoint: bfloat16 [5, 125, 65536], P(None, None, ('dom', 'sub'))
- shipped_primal: bfloat16 [5, 64, 65536], P(None, None, ('dom', 'sub'))
The draws below stay inside these ranges and needn't reach their ends.
Inputs may be any that keep to these rules, and one draw needn't show every extreme that they name: faces_nbr[f, e] is -1 for a boundary face; else w, and element floor(e / 2048) * 2048 + w - 256 exists. w < 256 only for f = 4 and e among the first 256 elements of its block; w >= 2304 only for f = 5 and e among the last 256 elements of its block. `move_elem`: the 256 entries of one device are distinct. `move_dest`: among the 256 moves of one device no destination is named more than 4 times.
All inputs are finite; a program needn't handle non-finite values.
Results may differ from the reference program's by a relative error of at most 0.0053.
Values may be sent and summed in bfloat16 or wider, within the bound.
A program may use at most 192 MiB of HBM per device.

```python
import math
import jax
import jax.numpy as jnp
import numpy as np
from jax import lax

NV = 5
NB = 64
NE = 125
NQ = 216
NF = 16
E_DEV = 2048
HALO = 256
MOV_DEV = 256
CAP = 4
ELEMS = 262144
MOVES = 32768
RECV = 65536
DEVICES = 128


def draw_primal(key, part):
    key = jax.random.fold_in(key, 11)
    ramp = 1.0 + 2.0 * jnp.arange(ELEMS, dtype=jnp.float32) / ELEMS
    values = jnp.clip(jax.random.normal(key, (NV, NB, ELEMS), jnp.float32), -4.0, 4.0) * ramp
    return values.astype(jnp.bfloat16)


def draw_faces_nbr(key, part):
    key = jax.random.fold_in(key, 23)
    key_inner, key_rim, key_live = jax.random.split(key, 3)
    glob = jnp.arange(ELEMS, dtype=jnp.int32)
    owner = glob // E_DEV
    local = glob % E_DEV
    inner = jax.random.randint(key_inner, (6, ELEMS), 0, E_DEV - 1)
    inner = jnp.where(inner >= local[None, :], inner + 1, inner)
    window = HALO + inner
    rim = jax.random.randint(key_rim, (6, ELEMS), 0, HALO)
    face = jnp.arange(6, dtype=jnp.int32)[:, None]
    lower = (face == 4) & (local[None, :] < HALO) & (owner[None, :] > 0)
    upper = (face == 5) & (local[None, :] >= E_DEV - HALO) & (owner[None, :] < DEVICES - 1)
    window = jnp.where(lower, rim, window)
    window = jnp.where(upper, HALO + E_DEV + rim, window)
    present = jax.random.randint(key_live, (6, ELEMS), 0, 8) > 0
    return jnp.where(present, window, -1).astype(jnp.int32)


def draw_move_elem(key, part):
    key = jax.random.fold_in(key, 37)
    keys = jax.random.split(key, DEVICES)
    picks = jax.vmap(lambda single: jax.random.permutation(single, E_DEV)[:MOV_DEV])(keys)
    return picks.reshape(MOVES).astype(jnp.int32)


def plant(drawn, own_key, least, top_value):
    dims = drawn.shape
    place = [jax.random.randint(jax.random.fold_in(own_key, axis), (), 0, dims[axis]) for axis in range(len(dims))]
    drawn = drawn.at[tuple(place)].set(least)
    longest = dims.index(max(dims))
    place[longest] = (place[longest] + 1) % dims[longest]
    return drawn.at[tuple(place)].set(top_value)


def steps_of(key, dims, shards, smallest, high):
    factor_of, own = 1.0, jax.random.fold_in(key, 6)
    for position, blocks in shards:
        draws = jnp.exp(jax.random.uniform(jax.random.fold_in(own, position), (blocks,), jnp.float32, smallest / len(shards), high / len(shards)))
        factor_of = factor_of * jnp.repeat(draws, dims[position] // blocks).reshape([-1 if axis == position else 1 for axis in range(len(dims))])
    return factor_of


def shared_out(stream_key, own, number, rows, amount, top, most, lean):
    ranking = jax.random.permutation(stream_key, amount)
    heavy_load, common = portions_of(amount, rows * top, most, lean, True), portions_of(amount, rows * top, most, lean, False)
    places = jnp.arange(amount)

    def named(lengths, offset_by):
        used = int((lengths > 0).sum())
        fixed = max(1, used // 4)
        passed = fixed + (places - fixed + offset_by * (used - fixed)) % max(1, amount - fixed)
        return jnp.zeros((amount,), jnp.int32).at[ranking[jnp.where(places < fixed, places, passed)]].set(jnp.asarray(lengths, jnp.int32))

    lengths = jnp.where(number % 4 == 0, named(heavy_load, number // 4), named(common, number - number // 4 - 1))
    mixed = jax.random.permutation(jax.random.fold_in(own, 3), amount)
    donor, taker = mixed[0:amount // 2 * 2:2], mixed[1:amount // 2 * 2:2]
    margin = jnp.minimum(lengths[donor] - 1, most - lengths[taker]) // 2
    margin = jnp.where((donor == ranking[0]) | (taker == ranking[0]) | (lengths[taker] == 0), 0, jnp.maximum(margin, 0))
    passed = jax.random.randint(jax.random.fold_in(own, 4), (amount // 2,), 0, 1 << 20) % (margin + 1)
    lengths = lengths.at[donor].add(-passed).at[taker].add(passed)
    labels = jnp.searchsorted(jnp.cumsum(lengths), jnp.arange(rows * top), side="right").astype(jnp.int32)
    listing = labels.reshape(top, rows).T
    listing = listing[jax.random.permutation(jax.random.fold_in(own, 1), rows)]
    offset_by = jax.random.randint(jax.random.fold_in(own, 2), (rows, 1), 0, top)
    return jnp.take_along_axis(listing, (jnp.arange(top)[None, :] + offset_by) % top, axis=1)


def portions_of(number_of, total, reach, skew, full):
    loads = [(1 << 20) // math.isqrt(rank ** skew) + 1 for rank in range(1, number_of + 1)]
    largest = reach if full else min(reach, max(-(-total // number_of), total * loads[0] // sum(loads)))
    least = 1 if total - largest >= number_of - 1 else 0
    given, rest = [largest] + [least] * (number_of - 1), total - largest - least * (number_of - 1)
    while rest > 0:
        free = [i for i in range(1, number_of) if given[i] < largest] or [i for i in range(1, number_of) if given[i] < reach]
        mass, budget = sum([loads[i] for i in free]), rest
        for i in free:
            addition = min(reach - given[i], max(1, budget * loads[i] // mass), rest)
            given[i] = given[i] + addition
            rest = rest - addition
    return np.array(given)


def gaussian(key, shape, deviation, most, pieces=(), held_as=jnp.bfloat16):
    drawn = deviation * jax.random.normal(key, shape, jnp.float32)
    if pieces:
        drawn = drawn * steps_of(key, shape, pieces, -0.22, 0.18)
    return jnp.clip(drawn, -most, most).astype(held_as)


def setup_inputs(seed: int = 0) -> dict:
    arg_keys = jax.random.split(jax.random.key(seed), 14)
    primal = draw_primal(jax.random.fold_in(arg_keys[13], 71), 0)
    adjoint = gaussian(arg_keys[1], (NV, NB, ELEMS), 1.0, 5.0, ((2, 128),))
    order = plant(jax.random.randint(arg_keys[2], (ELEMS,), 1, 4), jax.random.fold_in(arg_keys[2], 1), 1, 3).astype(jnp.int32)
    faces_nbr = draw_faces_nbr(jax.random.fold_in(arg_keys[13], 71), 0)
    move_elem = draw_move_elem(jax.random.fold_in(arg_keys[13], 71), 0)
    move_dest_keys = jax.random.split(jax.random.fold_in(arg_keys[5], 1), MOVES // MOV_DEV)
    move_dest_turns = jax.random.permutation(jax.random.fold_in(arg_keys[5], 3), MOVES // MOV_DEV)
    move_dest = jax.vmap(lambda own, number: shared_out(jax.random.fold_in(arg_keys[5], 2), own, number, MOV_DEV, DEVICES, 1, CAP, 2))(move_dest_keys, move_dest_turns).reshape((MOVES, 1))
    eval_op = gaussian(arg_keys[6], (NQ, NB), NB ** -0.5, 0.75)
    gradient_operator = gaussian(arg_keys[7], (3, NE, NQ), (3 * NQ) ** -0.5, 0.25)
    flux_jac = gaussian(arg_keys[8], (3, NV, NV), NV ** -0.5, 2.5, (), jnp.float32)
    trace_op = gaussian(arg_keys[9], (6, NF, NB), NB ** -0.5, 0.75)
    lifting_operator = gaussian(arg_keys[10], (6, NE, NF), (6 * NF) ** -0.5, 0.625)
    patch_from_self = gaussian(arg_keys[11], (NE, NB), NB ** -0.5, 0.75)
    patch_from_faces = gaussian(arg_keys[12], (6, NE, NF), (6 * NF) ** -0.5, 0.625)
    return dict(primal=primal, adjoint=adjoint, order=order, faces_nbr=faces_nbr, move_elem=move_elem, move_dest=move_dest, eval_op=eval_op, gradient_operator=gradient_operator, flux_jac=flux_jac, trace_op=trace_op, lifting_operator=lifting_operator, patch_from_self=patch_from_self, patch_from_faces=patch_from_faces)


def mode_degree(per_side):
    modes = jnp.arange(per_side ** 3, dtype=jnp.int32)
    deg_one = modes // (per_side * per_side)
    deg_two = (modes // per_side) % per_side
    deg_three = modes % per_side
    return jnp.maximum(jnp.maximum(deg_one, deg_two), deg_three)


def lookup(windows, neighbours):
    gathered = []
    for face in range(6):
        index = neighbours[face]
        picked = jnp.take(windows[face ^ 1], jnp.maximum(index, 0), axis=-1)
        gathered.append(jnp.where(index[None, None, None, :] >= 0, picked, jnp.zeros_like(picked)))
    return jnp.stack(gathered, axis=2)


def to_blocks(array):
    shaped = array.reshape(array.shape[:-1] + (DEVICES, E_DEV))
    return jnp.moveaxis(shaped, -2, 0)


def reference(primal, adjoint, order, faces_nbr, move_elem, move_dest, eval_op, gradient_operator, flux_jac, trace_op, lifting_operator, patch_from_self, patch_from_faces):
    keep_low = (mode_degree(4)[:, None] <= order[None, :]).astype(jnp.bfloat16)
    primal_blocks = to_blocks(primal * keep_low[None])
    adjoint_blocks = to_blocks(adjoint * keep_low[None])
    order_blocks = order.reshape(DEVICES, E_DEV)
    nbr_blocks = jnp.moveaxis(faces_nbr.reshape(6, DEVICES, E_DEV), 1, 0)

    def traces_of(pair):
        both = jnp.stack([pair[0], pair[1]]).astype(jnp.float32)
        return jnp.einsum("fnb,kvbe->kvfne", trace_op.astype(jnp.float32), both).astype(jnp.bfloat16)

    trace_blocks = lax.map(traces_of, (primal_blocks, adjoint_blocks))

    def element_work(items):
        device, prim, adjoint_field, order_blk, nbr, interior_trace = items
        keep_high = (mode_degree(5)[:, None] <= order_blk[None, :] + 1).astype(jnp.float32)
        lower_src = trace_blocks[jnp.maximum(device - 1, 0)][..., E_DEV - HALO:]
        lower = jnp.where(device > 0, lower_src, jnp.zeros_like(lower_src))
        upper_src = trace_blocks[jnp.minimum(device + 1, DEVICES - 1)][..., :HALO]
        upper = jnp.where(device < DEVICES - 1, upper_src, jnp.zeros_like(upper_src))
        window = jnp.concatenate([lower, interior_trace, upper], axis=-1)
        exterior_trace = lookup([window[:, :, face] for face in range(6)], nbr)
        enriched_adjoint = jnp.einsum("pq,cqk->cpk", patch_from_self.astype(jnp.float32), adjoint_field.astype(jnp.float32))
        enriched_adjoint = enriched_adjoint + jnp.einsum("yzu,hyui->hzi", patch_from_faces.astype(jnp.float32), exterior_trace[1].astype(jnp.float32))
        enriched_adjoint = (keep_high[None] * enriched_adjoint).astype(jnp.bfloat16)
        values = jnp.einsum("qb,vbe->vqe", eval_op.astype(jnp.float32), prim.astype(jnp.float32))
        fluxes = []
        for direction in range(3):
            mixed = jnp.einsum("uv,vqe->uqe", flux_jac[direction], values, precision=lax.Precision.HIGHEST)
            fluxes.append(mixed + 0.25 * values[direction + 1][None] * values)
        flux_every_face = jnp.stack(fluxes).astype(jnp.bfloat16)
        residual_values = jnp.einsum("lgy,luyc->ugc", gradient_operator.astype(jnp.float32), flux_every_face.astype(jnp.float32))
        residual_values = residual_values + jnp.einsum("yzu,hyui->hzi", lifting_operator.astype(jnp.float32), interior_trace[0].astype(jnp.float32))
        residual_values = residual_values - jnp.einsum("yzu,hyui->hzi", lifting_operator.astype(jnp.float32), exterior_trace[0].astype(jnp.float32))
        eta = jnp.abs(jnp.sum(enriched_adjoint.astype(jnp.float32) * residual_values, axis=(0, 1)))
        return eta, enriched_adjoint

    devices_idx = jnp.arange(DEVICES, dtype=jnp.int32)
    etas, enriched_blocks = lax.map(element_work, (devices_idx, primal_blocks, adjoint_blocks, order_blocks, nbr_blocks, trace_blocks))
    total = jnp.sum(etas)
    indicator = (etas * ELEMS / total).reshape(ELEMS)

    target = move_dest[:, 0].reshape(DEVICES, MOV_DEV)
    onehot = (target[:, :, None] == jnp.arange(DEVICES, dtype=jnp.int32)[None, None, :]).astype(jnp.int32)
    rank = jnp.sum((jnp.cumsum(onehot, axis=1) - onehot) * onehot, axis=-1)
    source = devices_idx[:, None]
    column = (target * (DEVICES * CAP) + source * CAP + rank).reshape(MOVES)
    elems = move_elem.reshape(DEVICES, MOV_DEV)
    adjoint_moved = enriched_blocks[source, :, :, elems].reshape(MOVES, NV * NE).T
    primal_moved = primal.reshape(NV * NB, ELEMS)[:, (source * E_DEV + elems).reshape(MOVES)]
    shipped_adjoint = jnp.zeros((NV * NE, RECV), jnp.bfloat16).at[:, column].set(adjoint_moved).reshape(NV, NE, RECV)
    shipped_primal = jnp.zeros((NV * NB, RECV), jnp.bfloat16).at[:, column].set(primal_moved).reshape(NV, NB, RECV)
    return (indicator, shipped_adjoint, shipped_primal)
```

```python
import jax
import jax.numpy as jnp
from jax import lax
from jax.experimental import pallas as pl
from jax.experimental.pallas import tpu as pltpu
from jax.sharding import PartitionSpec as P

AXES = ("dom", "sub")
F32 = jnp.float32
BF16 = jnp.bfloat16
VMEM = pl.BlockSpec(memory_space=pltpu.VMEM)
SMEM = pl.BlockSpec(memory_space=pltpu.SMEM)
ANY = pl.BlockSpec(memory_space=pl.ANY)
CHUNK = 256
LIMIT = 56 * 1024 * 1024


def dot(a, b):
    return jnp.dot(a, b, preferred_element_type=F32)


def dot_nt(a, b):
    return lax.dot_general(a, b, (((1,), (1,)), ((), ())), preferred_element_type=F32)


def dot_tn(a, b):
    return lax.dot_general(a, b, (((0,), (0,)), ((), ())), preferred_element_type=F32)


def one_hot(row, depth):
    rows = lax.broadcasted_iota(jnp.int32, (depth, row.shape[1]), 0).astype(jnp.int16)
    return jnp.where(rows == row.astype(jnp.int16), jnp.ones((), BF16), jnp.zeros((), BF16))


def span(c, width=CHUNK):
    return pl.ds(pl.multiple_of(c * width, width), width)


def mode_degree(per_side, shape):
    modes = lax.broadcasted_iota(jnp.int32, shape, 0)
    deg_one = modes // (per_side * per_side)
    deg_two = modes // per_side % per_side
    deg_three = modes % per_side
    return jnp.maximum(jnp.maximum(deg_one, deg_two), deg_three)


def main_kernel(
    groups,
    members,
    primal_in,
    adjoint_in,
    order,
    neighbours_in,
    elem_row,
    dest_row,
    self_t,
    faces_t,
    eval_t,
    slope_t,
    lift_t,
    trace_op,
    jacobian,
    received,
    error,
    total,
    primal,
    adjoint,
    neighbours,
    tall,
    wide,
    trace_mix,
    patch,
    evaluate,
    lifted,
    solo,
    paired,
    weights,
    traces,
    halo,
    outside,
    enriched,
    moved,
    send,
    values,
    moments,
    solo_moments,
    pair_moments,
    part,
    sums,
    loaded,
    halo_sent,
    halo_got,
    ship_sent,
    ship_got,
    sum_sent,
    sum_got,
    own_done,
):
    variables, modes, count = primal.shape
    high_count = self_t.shape[1]
    high_modes = enriched.shape[1]
    quad = eval_t.shape[1]
    padded = evaluate.shape[0]
    stacked = trace_op.shape[0]
    points = stacked // 6
    half = variables * points
    chunks = count // CHUNK
    devices = groups * members
    moves = elem_row.shape[1]
    slots = 4 * devices
    faces = 3 * padded
    share = devices // chunks
    step = 32
    pairs = ((1, 2), (2, 3), (1, 3))

    dom = lax.axis_index("dom")
    sub = lax.axis_index("sub")
    me = dom * members + sub

    def peer(offset):
        other = lax.rem(me + offset, devices)
        return other, (lax.div(other, members), lax.rem(other, members))

    def for_peers(c, act):
        for i in range(1, share):
            act(c * share + i)

        @pl.when(c < chunks - 1)
        def _():
            act(c * share + share)

    barrier = pltpu.get_barrier_semaphore()
    loads = [
        pltpu.make_async_copy(source, target, loaded.at[i])
        for i, (source, target) in enumerate(
            ((adjoint_in, adjoint), (primal_in, primal), (neighbours_in, neighbours))
        )
    ]
    for load in loads:
        load.start()

    @pl.loop(1, devices)
    def _(i):
        pl.semaphore_signal(barrier, inc=1, device_id=peer(i)[1])

    tall[...] = jnp.zeros_like(tall)
    tall[0:modes, 0:high_count] = self_t[...].astype(F32)
    tall[modes : modes + stacked, 0:high_count] = faces_t[...].astype(F32)
    patch[...] = tall[...].T.astype(BF16)
    trace_mix[...] = jnp.zeros_like(trace_mix)
    for v in range(4):
        trace_mix[v * stacked : (v + 1) * stacked, v * modes : (v + 1) * modes] = trace_op[...]

    low = mode_degree(4, (modes, CHUNK))
    high = mode_degree(5, (high_modes, CHUNK))

    def keep_low(at):
        return (low <= order[:, at]).astype(F32).astype(BF16)

    def trace(c, kind):
        at = pl.ds(c * CHUNK, CHUNK) if isinstance(c, int) else span(c)
        keep = keep_low(at)
        fields = [(primal, adjoint)[kind][v, :, at] * keep for v in range(variables)]
        for first in range(0, variables, 4):
            group = fields[first : first + 4]
            mixed = dot(
                trace_mix[: len(group) * stacked, : len(group) * modes],
                jnp.concatenate(group, axis=0) if len(group) > 1 else group[0],
            ).astype(BF16)
            for g in range(len(group)):
                row = (kind * variables + first + g) * points
                for f in range(6):
                    start = g * stacked + f * points
                    traces[f, c, row : row + points, :] = mixed[start : start + points]

    def halo_copy(side):
        return pltpu.make_async_remote_copy(
            src_ref=traces.at[5, chunks - 1] if side == 0 else traces.at[4, 0],
            dst_ref=halo.at[side],
            send_sem=halo_sent.at[side],
            recv_sem=halo_got.at[side],
            device_id=peer(1 if side == 0 else devices - 1)[1],
        )

    def gather(c, kind):
        at = span(c)
        for f in range(6):
            index = neighbours[f : f + 1, at] - CHUNK
            block = (index >> 8).astype(jnp.int16)
            table = traces[f ^ 1, :, kind * half : (kind + 1) * half, :]
            table = table.reshape(chunks * half, CHUNK)
            found = dot(table, one_hot(index & (CHUNK - 1), CHUNK)).astype(BF16)
            picked = jnp.zeros((half, CHUNK), BF16)
            for a in range(chunks):
                here = block == jnp.int16(a)
                picked = jnp.where(here, found[a * half : (a + 1) * half], picked)
            for v in range(variables):
                outside[kind * variables + v, f * points : (f + 1) * points, at] = picked[
                    v * points : (v + 1) * points
                ]

    def gather_halo(kind):
        for side, f, start, wanted in ((0, 4, 0, -1), (1, 5, count - CHUNK, chunks)):
            index = neighbours[f : f + 1, start : start + CHUNK] - CHUNK
            found = dot(halo[side, kind * half : (kind + 1) * half, :], one_hot(index & (CHUNK - 1), CHUNK))
            found = jnp.where((index >> 8) == wanted, found, 0.0).astype(BF16)
            for v in range(variables):
                place = (
                    kind * variables + v,
                    pl.ds(f * points, points),
                    pl.ds(start, CHUNK),
                )
                outside[place] = outside[place] + found[v * points : (v + 1) * points]

    named = one_hot(dest_row[...], devices)
    earlier = lax.broadcasted_iota(jnp.int32, (moves, moves), 0) < lax.broadcasted_iota(
        jnp.int32, (moves, moves), 1
    )
    before = dot(named, earlier.astype(F32).astype(BF16))
    rank = jnp.sum(before * named.astype(F32), axis=0, keepdims=True).astype(jnp.int32)
    slot = dest_row[...] * 4 + rank
    block_of = (elem_row[...] >> 8).astype(jnp.int16)
    low_of = elem_row[...] & (CHUNK - 1)

    def move(rows_of):
        pick = one_hot(low_of, CHUNK)
        held = None
        for a in range(chunks):
            found = dot(rows_of(pl.ds(a * CHUNK, CHUNK)), pick).astype(BF16)
            held = jnp.zeros_like(found) if held is None else held
            held = jnp.where(block_of == jnp.int16(a), found, held)
        return held

    def ship(i):
        other, target = peer(i)
        return pltpu.make_async_remote_copy(
            src_ref=send.at[other],
            dst_ref=received.at[me],
            send_sem=ship_sent,
            recv_sem=ship_got,
            device_id=target,
        )

    loads[0].wait()

    @pl.loop(0, chunks // 2)
    def _(c):
        for b in range(2):
            trace(2 * c + b, 1)

    loads[1].wait()
    loads[2].wait()
    trace(0, 0)
    trace(chunks - 1, 0)

    primal_rows = variables * high_modes
    moved[primal_rows : primal_rows + variables * modes, :] = move(
        lambda at: primal[:, :, at].reshape(variables * modes, CHUNK)
    )
    moved[primal_rows + variables * modes :, :] = jnp.zeros(
        (moved.shape[0] - primal_rows - variables * modes, moves), BF16
    )

    pl.semaphore_wait(barrier, devices - 1)
    for side in range(2):
        halo_copy(side).start()

    @pl.loop(0, chunks)
    def _(c):
        gather(c, 1)

    for side in range(2):
        halo_copy(side).wait_recv()
    gather_halo(1)

    def enrich(c):
        at = span(c)
        keep = keep_low(at)
        keep_high = (high <= order[:, at] + 1).astype(F32)
        for v in range(variables):
            own = adjoint[v, :, at] * keep
            both = jnp.concatenate([own, outside[variables + v, :, at]], axis=0)
            enriched[v, :, at] = (keep_high * dot(patch[:, : modes + stacked], both)).astype(BF16)

    @pl.loop(0, chunks // 2)
    def _(c):
        for b in range(2):
            enrich(2 * c + b)

    moved[:primal_rows, :] = move(
        lambda at: enriched[:, :, at].reshape(variables * high_modes, CHUNK)
    )
    place = one_hot(slot, slots)
    for j in range(0, 8, 2):
        pair = dot_nt(place, moved[j * 128 : (j + 2) * 128, :])
        for h in range(2):
            block = pair[:, h * 128 : (h + 1) * 128].reshape(devices, 4, 128)
            send[:, j + h] = block.astype(BF16)
    own = pltpu.make_async_copy(send.at[me], received.at[me], own_done)
    own.start()

    @pl.loop(0, chunks)
    def _(c):
        for_peers(c, lambda i: ship(i).start())

    @pl.loop(0, chunks // 2 - 1)
    def _(c):
        for b in range(2):
            trace(2 * c + 1 + b, 0)

    @pl.loop(0, chunks)
    def _(c):
        gather(c, 0)

    gather_halo(0)

    wide[...] = jnp.zeros_like(wide)
    wide[0:modes, 0:quad] = eval_t[...].astype(F32)
    evaluate[...] = wide[...].T[:padded, :modes].astype(BF16)
    lifted[...] = jnp.zeros_like(lifted)
    for d in range(3):
        lifted[d * padded : d * padded + quad, 0:high_count] = slope_t[d]
    lifted[faces : faces + stacked, 0:high_count] = lift_t[...]
    for d in range(3):
        solo[d, :padded, :] = lifted[d * padded : (d + 1) * padded, :]
        solo[d, padded:, :] = lifted[faces:, :]
    for p, (i, j) in enumerate(pairs):
        paired[p, :, :high_modes] = lifted[(j - 1) * padded : j * padded, :]
        paired[p, :, high_modes:] = lifted[(i - 1) * padded : i * padded, :]

    direct = dot_tn(trace_op[...], lifted[faces : faces + stacked, :])
    slopes = [dot(eval_t[...], lifted[d * padded : d * padded + quad, :]) for d in range(3)]
    for v in range(variables):
        for u in range(variables):
            block = jacobian[u, 0, v] * slopes[0]
            for d in range(1, 3):
                block = block + jacobian[u, d, v] * slopes[d]
            if u == v:
                block = block + direct
            weights[v * modes : (v + 1) * modes, u * high_modes : (u + 1) * high_modes] = (
                block.astype(BF16)
            )

    def errors(c, values, moments, solo_moments, pair_moments):
        at = span(c)
        keep = keep_low(at)
        every = enriched[:, :, at].reshape(variables * high_modes, CHUNK)
        linear = dot(weights[...], every)
        summed = jnp.zeros((step, CHUNK), F32)
        for v in range(variables):
            own = primal[v, :, at] * keep
            values[v] = dot(evaluate[...], own)
            for r in range(0, modes, step):
                summed = summed + own[r : r + step].astype(F32) * linear[
                    v * modes + r : v * modes + r + step
                ]
        for e, u in enumerate((0, 4)):
            moments[e] = dot(lifted[...], enriched[u, :, at])
        for u in range(1, 4):
            solo_moments[u - 1] = dot(solo[u - 1], enriched[u, :, at])
        for p, (i, j) in enumerate(pairs):
            both = jnp.concatenate([enriched[i, :, at], enriched[j, :, at]], axis=0)
            pair_moments[p] = dot(paired[p], both)
        for r in range(0, stacked, step):
            for u in range(variables):
                if u in (0, 4):
                    lift = moments[u // 4, faces + r : faces + r + step]
                else:
                    lift = solo_moments[u - 1, padded + r : padded + r + step]
                summed = summed - outside[u, r : r + step, at].astype(F32) * lift
        for r in range(0, padded, step):
            here = [values[v, r : r + step] for v in range(variables)]
            for d in range(3):
                row = d * padded + r
                inner = here[0] * moments[0, row : row + step]
                inner = inner + here[4] * moments[1, row : row + step]
                inner = inner + here[d + 1] * solo_moments[d, r : r + step]
                for p, (i, j) in enumerate(pairs):
                    if i == d + 1:
                        inner = inner + here[j] * pair_moments[p, r : r + step]
                summed = summed + (0.25 * here[d + 1]) * inner
        error[:, at] = jnp.abs(jnp.sum(summed, axis=0, keepdims=True))

    @pl.loop(0, chunks // 2)
    def _(c):
        for b in range(2):
            errors(2 * c + b, values.at[b], moments.at[b], solo_moments.at[b], pair_moments.at[b])

    mine = error[:, 0:128]
    for r in range(128, count, 128):
        mine = mine + error[:, r : r + 128]
    part[...] = mine
    sums[me] = mine

    def tell(i):
        return pltpu.make_async_remote_copy(
            src_ref=part,
            dst_ref=sums.at[me],
            send_sem=sum_sent,
            recv_sem=sum_got,
            device_id=peer(i)[1],
        )

    @pl.loop(1, devices)
    def _(i):
        tell(i).start()

    def every_other(ref, sent, got):
        others = ref.at[pl.ds(0, devices - 1)]
        return pltpu.make_async_remote_copy(
            src_ref=others, dst_ref=others, send_sem=sent, recv_sem=got, device_id=peer(1)[1]
        )

    waits = [
        every_other(received, ship_sent, ship_got),
        every_other(sums, sum_sent, sum_got),
    ]
    own.wait()
    for wait in waits:
        wait.wait_recv()
    whole = jnp.sum(jnp.sum(sums[...], axis=0), axis=1, keepdims=True)
    total[...] = jnp.broadcast_to(whole, total.shape)
    for wait in waits:
        wait.wait_send()
    for side in range(2):
        halo_copy(side).wait_send()


def unpack_kernel(
    elements, received, error, total, indicator, shipped_adjoint, shipped_primal
):
    variables, high_modes, slots = shipped_adjoint.shape
    modes = shipped_primal.shape[1]
    share = error[...] * elements / total[:, 0:1]
    for r in range(indicator.shape[0]):
        indicator[r : r + 1, :] = share[:, r * 128 : (r + 1) * 128]

    def columns(j):
        return received[:, j].astype(F32).reshape(slots, 128).T.astype(BF16)

    for j in range(variables):
        shipped_adjoint[j] = columns(j)[:high_modes]
    for j in range(3):
        block = columns(variables + j)
        shipped_primal[2 * j] = block[:modes]
        if 2 * j + 1 < variables:
            shipped_primal[2 * j + 1] = block[modes:]


def call(kernel, out_shape, in_specs, out_specs, scratch=(), **params):
    return pl.pallas_call(
        kernel,
        out_shape=out_shape,
        in_specs=in_specs,
        out_specs=out_specs,
        scratch_shapes=scratch,
        compiler_params=pltpu.CompilerParams(vmem_limit_bytes=LIMIT, **params),
    )


def body(
    primal,
    adjoint,
    order,
    faces_nbr,
    move_elem,
    move_dest,
    eval_op,
    gradient_operator,
    flux_jac,
    trace_op,
    lifting_operator,
    patch_from_self,
    patch_from_faces,
):
    variables, modes, count = primal.shape
    points = trace_op.shape[1]
    stacked = 6 * points
    half = variables * points
    chunks = count // CHUNK
    groups = lax.axis_size("dom")
    members = lax.axis_size("sub")
    devices = groups * members
    moves = move_elem.shape[0]
    slots = 4 * devices
    high = patch_from_self.shape[0]
    high_pad = 128
    quad_pad = 224
    shape = jax.ShapeDtypeStruct
    dma = pltpu.SemaphoreType.DMA

    received, error, total = call(
        lambda *refs: main_kernel(groups, members, *refs),
        (
            shape((devices, 8, 4, 128), BF16),
            shape((1, count), F32),
            shape((1, 128), F32),
        ),
        [ANY, ANY, VMEM, ANY] + [VMEM] * 8 + [SMEM],
        [ANY, VMEM, VMEM],
        [
            pltpu.VMEM(primal.shape, BF16),
            pltpu.VMEM(adjoint.shape, BF16),
            pltpu.VMEM(faces_nbr.shape, jnp.int32),
            pltpu.VMEM((256, high_pad), F32),
            pltpu.VMEM((128, 256), F32),
            pltpu.VMEM((4 * stacked, 4 * modes), BF16),
            pltpu.VMEM((high_pad, 256), BF16),
            pltpu.VMEM((quad_pad, modes), BF16),
            pltpu.VMEM((3 * quad_pad + stacked, high_pad), BF16),
            pltpu.VMEM((3, quad_pad + stacked, high_pad), BF16),
            pltpu.VMEM((3, quad_pad, 2 * high_pad), BF16),
            pltpu.VMEM((variables * modes, variables * high_pad), BF16),
            pltpu.VMEM((6, chunks, 2 * half, CHUNK), BF16),
            pltpu.VMEM((2, 2 * half, CHUNK), BF16),
            pltpu.VMEM((2 * variables, stacked, count), BF16),
            pltpu.VMEM((variables, high_pad, count), BF16),
            pltpu.VMEM((1024, moves), BF16),
            pltpu.VMEM((devices, 8, 4, 128), BF16),
            pltpu.VMEM((2, variables, quad_pad, CHUNK), F32),
            pltpu.VMEM((2, 2, 3 * quad_pad + stacked, CHUNK), F32),
            pltpu.VMEM((2, 3, quad_pad + stacked, CHUNK), F32),
            pltpu.VMEM((2, 3, quad_pad, CHUNK), F32),
            pltpu.VMEM((1, 128), F32),
            pltpu.VMEM((devices, 1, 128), F32),
            dma((3,)),
            dma((2,)),
            dma((2,)),
            dma,
            dma,
            dma,
            dma,
            dma,
        ],
        collective_id=0,
        has_side_effects=True,
    )(
        primal,
        adjoint,
        order.reshape(1, count),
        faces_nbr,
        move_elem.reshape(1, moves),
        move_dest.reshape(1, moves),
        patch_from_self.T,
        patch_from_faces.transpose(0, 2, 1).reshape(stacked, high),
        eval_op.T,
        gradient_operator.transpose(0, 2, 1),
        lifting_operator.transpose(0, 2, 1).reshape(stacked, high),
        trace_op.reshape(stacked, modes),
        flux_jac.transpose(1, 0, 2),
    )

    indicator, shipped_adjoint, shipped_primal = call(
        lambda *refs: unpack_kernel(count * devices, *refs),
        (
            shape((count // 128, 128), F32),
            shape((variables, high, slots), BF16),
            shape((variables, modes, slots), BF16),
        ),
        [VMEM] * 3,
        [VMEM] * 3,
    )(received, error, total)
    return (indicator.reshape(count), shipped_adjoint, shipped_primal)


def solution(mesh):
    return jax.shard_map(
        body,
        mesh=mesh,
        in_specs=(
            P(None, None, AXES),
            P(None, None, AXES),
            P(AXES),
            P(None, AXES),
            P(AXES),
            P(AXES, None),
            P(),
            P(),
            P(),
            P(),
            P(),
            P(),
            P(),
        ),
        out_specs=(P(AXES), P(None, None, AXES), P(None, None, AXES)),
        check_vma=False,
    )
```

```python
import jax
import jax.numpy as jnp
from jax import lax
from jax.experimental import pallas as pl
from jax.experimental.pallas import tpu as pltpu
from jax.sharding import PartitionSpec as P

AXES = ("dom", "sub")
F32 = jnp.float32
BF16 = jnp.bfloat16
VMEM = pl.BlockSpec(memory_space=pltpu.VMEM)
SMEM = pl.BlockSpec(memory_space=pltpu.SMEM)
ANY = pl.BlockSpec(memory_space=pl.ANY)
CHUNK = 256
LIMIT = 56 * 1024 * 1024


def dot(a, b):
    return jnp.dot(a, b, preferred_element_type=F32)


def dot_nt(a, b):
    return lax.dot_general(a, b, (((1,), (1,)), ((), ())), preferred_element_type=F32)


def dot_tn(a, b):
    return lax.dot_general(a, b, (((0,), (0,)), ((), ())), preferred_element_type=F32)


def one_hot(row, depth):
    rows = lax.broadcasted_iota(jnp.int32, (depth, row.shape[1]), 0).astype(jnp.int16)
    return jnp.where(rows == row.astype(jnp.int16), jnp.ones((), BF16), jnp.zeros((), BF16))


def span(c, width=CHUNK):
    return pl.ds(pl.multiple_of(c * width, width), width)


def mode_degree(per_side, shape):
    modes = lax.broadcasted_iota(jnp.int32, shape, 0)
    deg_one = modes // (per_side * per_side)
    deg_two = modes // per_side % per_side
    deg_three = modes % per_side
    return jnp.maximum(jnp.maximum(deg_one, deg_two), deg_three)


def main_kernel(
    groups,
    members,
    primal_in,
    adjoint_in,
    order,
    neighbours_in,
    elem_row,
    dest_row,
    self_t,
    faces_t,
    eval_t,
    slope_t,
    lift_t,
    trace_op,
    jacobian,
    received,
    error,
    total,
    primal,
    adjoint,
    neighbours,
    tall,
    wide,
    trace_mix,
    patch,
    evaluate,
    lifted,
    solo,
    paired,
    weights,
    traces,
    halo,
    outside,
    enriched,
    moved,
    send,
    values,
    moments,
    solo_moments,
    pair_moments,
    part,
    sums,
    loaded,
    halo_sent,
    halo_got,
    ship_sent,
    ship_got,
    sum_sent,
    sum_got,
    own_done,
):
    variables, modes, count = primal.shape
    high_count = self_t.shape[1]
    high_modes = enriched.shape[1]
    quad = eval_t.shape[1]
    padded = evaluate.shape[0]
    stacked = trace_op.shape[0]
    points = stacked // 6
    half = variables * points
    chunks = count // CHUNK
    devices = groups * members
    moves = elem_row.shape[1]
    slots = 4 * devices
    faces = 3 * padded
    share = devices // chunks
    step = 32
    pairs = ((1, 2), (2, 3), (1, 3))

    dom = lax.axis_index("dom")
    sub = lax.axis_index("sub")
    me = dom * members + sub

    def peer(offset):
        other = lax.rem(me + offset, devices)
        return other, (lax.div(other, members), lax.rem(other, members))

    def for_peers(c, act):
        for i in range(1, share):
            act(c * share + i)

        @pl.when(c < chunks - 1)
        def _():
            act(c * share + share)

    barrier = pltpu.get_barrier_semaphore()
    loads = [
        pltpu.make_async_copy(source, target, loaded.at[i])
        for i, (source, target) in enumerate(
            ((adjoint_in, adjoint), (primal_in, primal), (neighbours_in, neighbours))
        )
    ]
    for load in loads:
        load.start()

    @pl.loop(1, devices)
    def _(i):
        pl.semaphore_signal(barrier, inc=1, device_id=peer(i)[1])

    tall[...] = jnp.zeros_like(tall)
    tall[0:modes, 0:high_count] = self_t[...].astype(F32)
    tall[modes : modes + stacked, 0:high_count] = faces_t[...].astype(F32)
    patch[...] = tall[...].T.astype(BF16)
    trace_mix[...] = jnp.zeros_like(trace_mix)
    for v in range(4):
        trace_mix[v * stacked : (v + 1) * stacked, v * modes : (v + 1) * modes] = trace_op[...]

    low = mode_degree(4, (modes, CHUNK))
    high = mode_degree(5, (high_modes, CHUNK))

    def keep_low(at):
        return (low <= order[:, at]).astype(F32).astype(BF16)

    def trace(c, kind):
        at = pl.ds(c * CHUNK, CHUNK) if isinstance(c, int) else span(c)
        keep = keep_low(at)
        fields = [(primal, adjoint)[kind][v, :, at] * keep for v in range(variables)]
        for first in range(0, variables, 4):
            group = fields[first : first + 4]
            mixed = dot(
                trace_mix[: len(group) * stacked, : len(group) * modes],
                jnp.concatenate(group, axis=0) if len(group) > 1 else group[0],
            ).astype(BF16)
            for g in range(len(group)):
                row = (kind * variables + first + g) * points
                for f in range(6):
                    start = g * stacked + f * points
                    traces[f, c, row : row + points, :] = mixed[start : start + points]

    def halo_copy(side):
        return pltpu.make_async_remote_copy(
            src_ref=traces.at[5, chunks - 1] if side == 0 else traces.at[4, 0],
            dst_ref=halo.at[side],
            send_sem=halo_sent.at[side],
            recv_sem=halo_got.at[side],
            device_id=peer(1 if side == 0 else devices - 1)[1],
        )

    def gather(c, kind):
        at = span(c)
        for f in range(6):
            index = neighbours[f : f + 1, at] - CHUNK
            block = (index >> 8).astype(jnp.int16)
            table = traces[f ^ 1, :, kind * half : (kind + 1) * half, :]
            table = table.reshape(chunks * half, CHUNK)
            found = dot(table, one_hot(index & (CHUNK - 1), CHUNK)).astype(BF16)
            picked = jnp.zeros((half, CHUNK), BF16)
            for a in range(chunks):
                here = block == jnp.int16(a)
                picked = jnp.where(here, found[a * half : (a + 1) * half], picked)
            for v in range(variables):
                outside[kind * variables + v, f * points : (f + 1) * points, at] = picked[
                    v * points : (v + 1) * points
                ]

    def gather_halo(kind):
        for side, f, start, wanted in ((0, 4, 0, -1), (1, 5, count - CHUNK, chunks)):
            index = neighbours[f : f + 1, start : start + CHUNK] - CHUNK
            found = dot(halo[side, kind * half : (kind + 1) * half, :], one_hot(index & (CHUNK - 1), CHUNK))
            found = jnp.where((index >> 8) == wanted, found, 0.0).astype(BF16)
            for v in range(variables):
                place = (
                    kind * variables + v,
                    pl.ds(f * points, points),
                    pl.ds(start, CHUNK),
                )
                outside[place] = outside[place] + found[v * points : (v + 1) * points]

    named = one_hot(dest_row[...], devices)
    earlier = lax.broadcasted_iota(jnp.int32, (moves, moves), 0) < lax.broadcasted_iota(
        jnp.int32, (moves, moves), 1
    )
    before = dot(named, earlier.astype(F32).astype(BF16))
    rank = jnp.sum(before * named.astype(F32), axis=0, keepdims=True).astype(jnp.int32)
    slot = dest_row[...] * 4 + rank
    block_of = (elem_row[...] >> 8).astype(jnp.int16)
    low_of = elem_row[...] & (CHUNK - 1)

    def move(rows_of):
        pick = one_hot(low_of, CHUNK)
        held = None
        for a in range(chunks):
            found = dot(rows_of(pl.ds(a * CHUNK, CHUNK)), pick).astype(BF16)
            held = jnp.zeros_like(found) if held is None else held
            held = jnp.where(block_of == jnp.int16(a), found, held)
        return held

    def ship(i):
        other, target = peer(i)
        return pltpu.make_async_remote_copy(
            src_ref=send.at[other],
            dst_ref=received.at[me],
            send_sem=ship_sent,
            recv_sem=ship_got,
            device_id=target,
        )

    loads[0].wait()

    @pl.loop(0, chunks // 2)
    def _(c):
        for b in range(2):
            trace(2 * c + b, 1)

    loads[1].wait()
    loads[2].wait()
    trace(0, 0)
    trace(chunks - 1, 0)

    primal_rows = variables * high_modes
    moved[primal_rows : primal_rows + variables * modes, :] = move(
        lambda at: primal[:, :, at].reshape(variables * modes, CHUNK)
    )
    moved[primal_rows + variables * modes :, :] = jnp.zeros(
        (moved.shape[0] - primal_rows - variables * modes, moves), BF16
    )

    pl.semaphore_wait(barrier, devices - 1)
    for side in range(2):
        halo_copy(side).start()

    @pl.loop(0, chunks // 2)
    def _(c):
        for b in range(2):
            gather(2 * c + b, 1)

    for side in range(2):
        halo_copy(side).wait_recv()
    gather_halo(1)

    def enrich(c):
        at = span(c)
        keep = keep_low(at)
        keep_high = (high <= order[:, at] + 1).astype(F32)
        for v in range(variables):
            own = adjoint[v, :, at] * keep
            both = jnp.concatenate([own, outside[variables + v, :, at]], axis=0)
            enriched[v, :, at] = (keep_high * dot(patch[:, : modes + stacked], both)).astype(BF16)

    @pl.loop(0, chunks // 2)
    def _(c):
        for b in range(2):
            enrich(2 * c + b)

    moved[:primal_rows, :] = move(
        lambda at: enriched[:, :, at].reshape(variables * high_modes, CHUNK)
    )
    place = one_hot(slot, slots)
    for j in range(0, 8, 2):
        pair = dot_nt(place, moved[j * 128 : (j + 2) * 128, :])
        for h in range(2):
            block = pair[:, h * 128 : (h + 1) * 128].reshape(devices, 4, 128)
            send[:, j + h] = block.astype(BF16)
    own = pltpu.make_async_copy(send.at[me], received.at[me], own_done)
    own.start()

    @pl.loop(0, chunks)
    def _(c):
        for_peers(c, lambda i: ship(i).start())

    @pl.loop(0, chunks // 2 - 1)
    def _(c):
        for b in range(2):
            trace(2 * c + 1 + b, 0)

    @pl.loop(0, chunks // 2)
    def _(c):
        for b in range(2):
            gather(2 * c + b, 0)

    gather_halo(0)

    wide[...] = jnp.zeros_like(wide)
    wide[0:modes, 0:quad] = eval_t[...].astype(F32)
    evaluate[...] = wide[...].T[:padded, :modes].astype(BF16)
    lifted[...] = jnp.zeros_like(lifted)
    for d in range(3):
        lifted[d * padded : d * padded + quad, 0:high_count] = slope_t[d]
    lifted[faces : faces + stacked, 0:high_count] = lift_t[...]
    for d in range(3):
        solo[d, :padded, :] = lifted[d * padded : (d + 1) * padded, :]
        solo[d, padded:, :] = lifted[faces:, :]
    for p, (i, j) in enumerate(pairs):
        paired[p, :, :high_modes] = lifted[(j - 1) * padded : j * padded, :]
        paired[p, :, high_modes:] = lifted[(i - 1) * padded : i * padded, :]

    direct = dot_tn(trace_op[...], lifted[faces : faces + stacked, :])
    slopes = [dot(eval_t[...], lifted[d * padded : d * padded + quad, :]) for d in range(3)]
    for v in range(variables):
        for u in range(variables):
            block = jacobian[u, 0, v] * slopes[0]
            for d in range(1, 3):
                block = block + jacobian[u, d, v] * slopes[d]
            if u == v:
                block = block + direct
            weights[v * modes : (v + 1) * modes, u * high_modes : (u + 1) * high_modes] = (
                block.astype(BF16)
            )

    def errors(c, values, moments, solo_moments, pair_moments):
        at = span(c)
        keep = keep_low(at)
        every = enriched[:, :, at].reshape(variables * high_modes, CHUNK)
        linear = dot(weights[...], every)
        summed = jnp.zeros((step, CHUNK), F32)
        for v in range(variables):
            own = primal[v, :, at] * keep
            values[v] = dot(evaluate[...], own)
            for r in range(0, modes, step):
                summed = summed + own[r : r + step].astype(F32) * linear[
                    v * modes + r : v * modes + r + step
                ]
        for e, u in enumerate((0, 4)):
            moments[e] = dot(lifted[...], enriched[u, :, at])
        for u in range(1, 4):
            solo_moments[u - 1] = dot(solo[u - 1], enriched[u, :, at])
        for p, (i, j) in enumerate(pairs):
            both = jnp.concatenate([enriched[i, :, at], enriched[j, :, at]], axis=0)
            pair_moments[p] = dot(paired[p], both)
        for r in range(0, stacked, step):
            for u in range(variables):
                if u in (0, 4):
                    lift = moments[u // 4, faces + r : faces + r + step]
                else:
                    lift = solo_moments[u - 1, padded + r : padded + r + step]
                summed = summed - outside[u, r : r + step, at].astype(F32) * lift
        for r in range(0, padded, step):
            here = [values[v, r : r + step] for v in range(variables)]
            for d in range(3):
                row = d * padded + r
                inner = here[0] * moments[0, row : row + step]
                inner = inner + here[4] * moments[1, row : row + step]
                inner = inner + here[d + 1] * solo_moments[d, r : r + step]
                for p, (i, j) in enumerate(pairs):
                    if i == d + 1:
                        inner = inner + here[j] * pair_moments[p, r : r + step]
                summed = summed + (0.25 * here[d + 1]) * inner
        error[:, at] = jnp.abs(jnp.sum(summed, axis=0, keepdims=True))

    @pl.loop(0, chunks // 2)
    def _(c):
        for b in range(2):
            errors(2 * c + b, values.at[b], moments.at[b], solo_moments.at[b], pair_moments.at[b])

    mine = error[:, 0:128]
    for r in range(128, count, 128):
        mine = mine + error[:, r : r + 128]
    part[...] = mine
    sums[me] = mine

    def tell(i):
        return pltpu.make_async_remote_copy(
            src_ref=part,
            dst_ref=sums.at[me],
            send_sem=sum_sent,
            recv_sem=sum_got,
            device_id=peer(i)[1],
        )

    @pl.loop(1, devices)
    def _(i):
        tell(i).start()

    def every_other(ref, sent, got):
        others = ref.at[pl.ds(0, devices - 1)]
        return pltpu.make_async_remote_copy(
            src_ref=others, dst_ref=others, send_sem=sent, recv_sem=got, device_id=peer(1)[1]
        )

    waits = [
        every_other(received, ship_sent, ship_got),
        every_other(sums, sum_sent, sum_got),
    ]
    own.wait()
    for wait in waits:
        wait.wait_recv()
    whole = jnp.sum(jnp.sum(sums[...], axis=0), axis=1, keepdims=True)
    total[...] = jnp.broadcast_to(whole, total.shape)
    for wait in waits:
        wait.wait_send()
    for side in range(2):
        halo_copy(side).wait_send()


def unpack_kernel(
    elements, received, error, total, indicator, shipped_adjoint, shipped_primal
):
    variables, high_modes, slots = shipped_adjoint.shape
    modes = shipped_primal.shape[1]
    share = error[...] * elements / total[:, 0:1]
    for r in range(indicator.shape[0]):
        indicator[r : r + 1, :] = share[:, r * 128 : (r + 1) * 128]

    def columns(j):
        return received[:, j].astype(F32).reshape(slots, 128).T.astype(BF16)

    for j in range(variables):
        shipped_adjoint[j] = columns(j)[:high_modes]
    for j in range(3):
        block = columns(variables + j)
        shipped_primal[2 * j] = block[:modes]
        if 2 * j + 1 < variables:
            shipped_primal[2 * j + 1] = block[modes:]


def call(kernel, out_shape, in_specs, out_specs, scratch=(), **params):
    return pl.pallas_call(
        kernel,
        out_shape=out_shape,
        in_specs=in_specs,
        out_specs=out_specs,
        scratch_shapes=scratch,
        compiler_params=pltpu.CompilerParams(vmem_limit_bytes=LIMIT, **params),
    )


def body(
    primal,
    adjoint,
    order,
    faces_nbr,
    move_elem,
    move_dest,
    eval_op,
    gradient_operator,
    flux_jac,
    trace_op,
    lifting_operator,
    patch_from_self,
    patch_from_faces,
):
    variables, modes, count = primal.shape
    points = trace_op.shape[1]
    stacked = 6 * points
    half = variables * points
    chunks = count // CHUNK
    groups = lax.axis_size("dom")
    members = lax.axis_size("sub")
    devices = groups * members
    moves = move_elem.shape[0]
    slots = 4 * devices
    high = patch_from_self.shape[0]
    high_pad = 128
    quad_pad = 224
    shape = jax.ShapeDtypeStruct
    dma = pltpu.SemaphoreType.DMA

    received, error, total = call(
        lambda *refs: main_kernel(groups, members, *refs),
        (
            shape((devices, 8, 4, 128), BF16),
            shape((1, count), F32),
            shape((1, 128), F32),
        ),
        [ANY, ANY, VMEM, ANY] + [VMEM] * 8 + [SMEM],
        [ANY, VMEM, VMEM],
        [
            pltpu.VMEM(primal.shape, BF16),
            pltpu.VMEM(adjoint.shape, BF16),
            pltpu.VMEM(faces_nbr.shape, jnp.int32),
            pltpu.VMEM((256, high_pad), F32),
            pltpu.VMEM((128, 256), F32),
            pltpu.VMEM((4 * stacked, 4 * modes), BF16),
            pltpu.VMEM((high_pad, 256), BF16),
            pltpu.VMEM((quad_pad, modes), BF16),
            pltpu.VMEM((3 * quad_pad + stacked, high_pad), BF16),
            pltpu.VMEM((3, quad_pad + stacked, high_pad), BF16),
            pltpu.VMEM((3, quad_pad, 2 * high_pad), BF16),
            pltpu.VMEM((variables * modes, variables * high_pad), BF16),
            pltpu.VMEM((6, chunks, 2 * half, CHUNK), BF16),
            pltpu.VMEM((2, 2 * half, CHUNK), BF16),
            pltpu.VMEM((2 * variables, stacked, count), BF16),
            pltpu.VMEM((variables, high_pad, count), BF16),
            pltpu.VMEM((1024, moves), BF16),
            pltpu.VMEM((devices, 8, 4, 128), BF16),
            pltpu.VMEM((2, variables, quad_pad, CHUNK), F32),
            pltpu.VMEM((2, 2, 3 * quad_pad + stacked, CHUNK), F32),
            pltpu.VMEM((2, 3, quad_pad + stacked, CHUNK), F32),
            pltpu.VMEM((2, 3, quad_pad, CHUNK), F32),
            pltpu.VMEM((1, 128), F32),
            pltpu.VMEM((devices, 1, 128), F32),
            dma((3,)),
            dma((2,)),
            dma((2,)),
            dma,
            dma,
            dma,
            dma,
            dma,
        ],
        collective_id=0,
        has_side_effects=True,
    )(
        primal,
        adjoint,
        order.reshape(1, count),
        faces_nbr,
        move_elem.reshape(1, moves),
        move_dest.reshape(1, moves),
        patch_from_self.T,
        patch_from_faces.transpose(0, 2, 1).reshape(stacked, high),
        eval_op.T,
        gradient_operator.transpose(0, 2, 1),
        lifting_operator.transpose(0, 2, 1).reshape(stacked, high),
        trace_op.reshape(stacked, modes),
        flux_jac.transpose(1, 0, 2),
    )

    indicator, shipped_adjoint, shipped_primal = call(
        lambda *refs: unpack_kernel(count * devices, *refs),
        (
            shape((count // 128, 128), F32),
            shape((variables, high, slots), BF16),
            shape((variables, modes, slots), BF16),
        ),
        [VMEM] * 3,
        [VMEM] * 3,
    )(received, error, total)
    return (indicator.reshape(count), shipped_adjoint, shipped_primal)


def solution(mesh):
    return jax.shard_map(
        body,
        mesh=mesh,
        in_specs=(
            P(None, None, AXES),
            P(None, None, AXES),
            P(AXES),
            P(None, AXES),
            P(AXES),
            P(AXES, None),
            P(),
            P(),
            P(),
            P(),
            P(),
            P(),
            P(),
        ),
        out_specs=(P(AXES), P(None, None, AXES), P(None, None, AXES)),
        check_vma=False,
    )
```
